768 devices in a mesh: row: 8 (over x, core), col: 12 (over z), state: 8 (over y).
Axes of the slice: x: 4, y: 8, z: 12, core: 2. Of those that a mesh axis runs over, the one named last changes fastest.
Arguments:
- vectors: bfloat16 [768, 4, 128, 128], P(('row', 'col')), may hold values from -6 to 6
- onsite: float32 [768, 128], P(('row', 'col'), 'state'), may hold values from 1 to 10
- k_tiles: bfloat16 [768, 16, 128, 128], P(('row', 'col'), 'state'), may hold values from -0.125 to 0.125
- s_tiles: bfloat16 [768, 16, 128, 128], P(('row', 'col'), 'state'), may hold values from -0.0625 to 0.0625
- columns: int32 [768, 16], P(('row', 'col')), may hold values from 0 to 767, as said below
- counts: int32 [768], P(('row', 'col')), may hold values from 2 to 16, as said below
Outputs:
- correction: float32 [768, 4, 128, 128], P(('row', 'col'), None, 'state')
- ritz: float32 [4], replicated
The draws below stay inside these ranges and needn't reach their ends.
Inputs may be any that keep to these rules, and one draw needn't show every extreme that they name: `columns`: the screened blocks of block row i lie in block rows between the first block row of i's device minus 8 and its last block row plus 8, inside the grid; each row lists distinct blocks, its own block in slot 0. `counts`: some block row has all 16 slots live.
All inputs are finite; a program needn't handle non-finite values.
Results may differ from the reference program's by a relative error of at most 0.025.
Values may be sent and summed in bfloat16 or wider, within the bound.
No kernel may reach another device: no remote copies, remote signals or barrier semaphores. Data moves between devices by JAX's collectives and lax.ppermute only.
A program may use at most 32 MiB of HBM per device.

```python
import math
import jax
import jax.numpy as jnp
from jax import lax

TILE = 128
NS = 4
MAXB = 16
REACH = 8
RB = 8
NB = 768


def draw_columns(key, part):
    key = jax.random.fold_in(key, 11)
    span = RB + 2 * REACH
    rows_all = jnp.arange(NB, dtype=jnp.int32)
    offsets = jnp.arange(span, dtype=jnp.int32)
    base = rows_all // RB * RB - REACH
    candidate = base[:, None] + offsets[None, :]
    valid = (candidate >= 0) & (candidate < NB)
    scores = jax.random.randint(key, (NB, span), 0, 1 << 20, dtype=jnp.int32) * span + offsets[None, :]
    scores = jnp.where(candidate == rows_all[:, None], jnp.int32(1 << 27), scores)
    scores = jnp.where(valid, scores, -1 - offsets[None, :])
    order = jnp.argsort(-scores, axis=1, stable=True)[:, :MAXB]
    return jnp.take_along_axis(candidate, order, axis=1).astype(jnp.int32)


def draw_counts(key, part):
    key = jax.random.fold_in(key, 23)
    first, second = jax.random.split(key)
    values = jax.random.randint(first, (NB,), 2, MAXB + 1, dtype=jnp.int32)
    where_full = jax.random.randint(second, (), 0, NB, dtype=jnp.int32)
    positions = jnp.arange(NB, dtype=jnp.int32)
    return jnp.where(positions == where_full, jnp.int32(MAXB), values).astype(jnp.int32)


def level_of(own_key, extent, cuts, least, largest):
    level = 1.0
    for dim, blocks in cuts:
        steps = jax.random.uniform(jax.random.fold_in(jax.random.fold_in(own_key, 6), dim), (blocks,), jnp.float32, least / len(cuts), largest / len(cuts))
        level = level * jnp.repeat(jnp.exp(steps), extent[dim] // blocks).reshape((-1,) + (1,) * (len(extent) - 1 - dim))
    return level


def bell_draw(key, dims, deviation, bound, shards=(), kind=jnp.bfloat16):
    values = deviation * jax.random.normal(key, dims, jnp.float32)
    if shards:
        values = values * level_of(key, dims, shards, -0.22, 0.18)
    return jnp.clip(values, -bound, bound).astype(kind)


def setup_inputs(seed: int = 0) -> dict:
    streams_of = jax.random.split(jax.random.key(seed), 7)
    vectors = bell_draw(streams_of[0], (NB, NS, TILE, TILE), 1.0, 6.0, ((0, 96),))
    onsite = jnp.clip(jnp.exp(math.log(10.0) - 2.3025851 * jax.random.uniform(streams_of[1], (NB, TILE), jnp.float32) ** level_of(streams_of[1], (NB, TILE), ((0, 96), (1, 8)), -0.2, 0.2)), 1.0, 10.0)
    k_tiles = bell_draw(streams_of[2], (NB, MAXB, TILE, TILE), (MAXB * TILE) ** -0.5, 0.125, ((0, 96), (1, 8)))
    s_tiles = bell_draw(streams_of[3], (NB, MAXB, TILE, TILE), (4 * MAXB * TILE) ** -0.5, 0.0625, ((0, 96), (1, 8)))
    columns = draw_columns(jax.random.fold_in(streams_of[6], 71), 0)
    counts = draw_counts(jax.random.fold_in(streams_of[6], 71), 0)
    return dict(vectors=vectors, onsite=onsite, k_tiles=k_tiles, s_tiles=s_tiles, columns=columns, counts=counts)


def reference(vectors, onsite, k_tiles, s_tiles, columns, counts):
    slots = lax.broadcasted_iota(jnp.int32, columns.shape, 1)
    live = (slots < counts[:, None]).astype(jnp.float32)

    def one_row(items):
        k_row, s_row, c_row, l_row = items
        blocks = jnp.take(vectors, c_row, axis=0).astype(jnp.float32)
        gate = l_row[:, None, None]
        k_part = jnp.einsum('mab,msbc->sac', k_row.astype(jnp.float32) * gate, blocks, precision=lax.Precision.HIGHEST)
        s_part = jnp.einsum('mab,msbc->sac', s_row.astype(jnp.float32) * gate, blocks, precision=lax.Precision.HIGHEST)
        return (k_part, s_part)
    coupled, intersected = lax.map(one_row, (k_tiles, s_tiles, columns, live))
    whole = vectors.astype(jnp.float32)
    kx = onsite[:, None, :, None] * whole + coupled
    sx = whole + intersected
    cross = lax.optimization_barrier(jnp.sum(sx * kx, axis=(0, 2, 3)))
    power = lax.optimization_barrier(jnp.sum(sx * sx, axis=(0, 2, 3)))
    ritz = cross / (power + 1e-06)
    resid = kx - ritz[None, :, None, None] * sx
    norm = lax.optimization_barrier(jnp.sum(resid * resid, axis=(0, 2, 3)))
    cells = vectors.shape[0] * vectors.shape[2] * vectors.shape[3]
    correction = resid * lax.rsqrt(norm / cells + 1e-06)[None, :, None, None]
    return (correction, ritz)
```

```python
import functools

import jax
import jax.numpy as jnp
from jax import lax
from jax.experimental import pallas as pl
from jax.experimental.pallas import tpu as pltpu
from jax.sharding import PartitionSpec as P

REACH = 8
EPS = 1e-06
VMEM = pl.BlockSpec(memory_space=pltpu.VMEM)
SMEM = pl.BlockSpec(memory_space=pltpu.SMEM)
LIMIT = 48 * 1024 * 1024


def lanes(values, width=128):
    lane = lax.broadcasted_iota(jnp.int32, (1, width), 1)
    row = jnp.zeros((1, width), jnp.float32)
    for k, value in enumerate(values):
        row = jnp.where(lane == k, value, row)
    return row


def product_kernel(
    states, place_ref, layer_ref, tiles_ref, low_ref, mid_ref, high_ref, onsite_ref,
    kx_ref, sx_ref, stat_ref, oper_ref,
):
    layers, _, rows_blk, slot_dev, own, width = tiles_ref.shape
    half = rows_blk * own
    span = low_ref.shape[0] + mid_ref.shape[0] + high_ref.shape[0]
    oper_ref[:, : span * width] = jnp.zeros((2 * half, span * width), oper_ref.dtype)
    for i in range(rows_blk):
        for y in range(layers):
            for m in range(slot_dev):
                at = pl.ds(pl.multiple_of(place_ref[i, y * slot_dev + m] * width, width), width)
                for op in range(2):
                    first = op * half + i * own
                    oper_ref[first : first + own, at] = tiles_ref[y, op, i, m]

    mine_at = pl.ds(pl.multiple_of(layer_ref[0] * own, own), own)
    diagonal = onsite_ref[...].reshape(half, width)
    power, cross, norm = [], [], []
    for s in range(0, states, 2):
        total = jnp.zeros((2 * half, 2 * width), jnp.float32)
        at = 0
        for ref in (low_ref, mid_ref, high_ref):
            depth = ref.shape[0] * width
            blocks = jnp.concatenate(
                [ref[:, t].reshape(depth, width) for t in (s, s + 1)], axis=1
            )
            total = total + jnp.dot(
                oper_ref[:, at : at + depth], blocks, preferred_element_type=jnp.float32
            )
            at += depth
        for t in range(2):
            mine = mid_ref[:, s + t, mine_at, :].astype(jnp.float32).reshape(half, width)
            coupled = total[:half, t * width : (t + 1) * width]
            intersected = total[half:, t * width : (t + 1) * width]
            kx = diagonal * mine + coupled
            sx = mine + intersected
            kx_ref[:, s + t] = kx.reshape(rows_blk, own, width)
            sx_ref[:, s + t] = sx.reshape(rows_blk, own, width)
            p = jnp.sum(sx * sx, keepdims=True)
            c = jnp.sum(sx * kx, keepdims=True)
            resid = kx - (c / (p + EPS)) * sx
            power.append(p)
            cross.append(c)
            norm.append(jnp.sum(resid * resid, keepdims=True))
    stat_ref[...] = jnp.broadcast_to(lanes(power + cross + norm)[None], stat_ref.shape)


def merged(parts, states):
    power = parts
    cross = pltpu.roll(parts, parts.shape[1] - states, 1)
    norm = pltpu.roll(parts, parts.shape[1] - 2 * states, 1)
    power_all = jnp.sum(power, axis=0, keepdims=True)
    cross_all = jnp.sum(cross, axis=0, keepdims=True)
    ratio = cross / (power + EPS)
    ritz = cross_all / (power_all + EPS)
    gap = ratio - ritz
    norm_all = jnp.sum(norm + (2 * EPS) * gap * ratio + gap * gap * power, axis=0, keepdims=True)
    return power_all, cross_all, norm_all, ritz


def pick(row, k):
    return row[:, k : k + 1]


def merge_kernel(states, parts_ref, stat_ref):
    power, cross, norm, _ = merged(parts_ref[...].reshape(parts_ref.shape[0], -1), states)
    row = lanes([pick(a, k) for a in (power, cross, norm) for k in range(states)])
    stat_ref[...] = jnp.broadcast_to(row[None], stat_ref.shape)


def final_kernel(states, cells, parts_ref, kx_ref, sx_ref, out_ref, ritz_ref):
    _, _, norm, ritz = merged(parts_ref[...].reshape(parts_ref.shape[0], -1), states)
    scale = lax.rsqrt(norm / cells + EPS)
    for s in range(states):
        out_ref[:, s] = (kx_ref[:, s] - pick(ritz, s)[None] * sx_ref[:, s]) * pick(scale, s)[None]
    ritz_ref[...] = ritz


def per_device(vectors, onsite, k_tiles, s_tiles, columns, counts):
    rows_blk, states, width, _ = vectors.shape
    layers = lax.axis_size("state")
    layer = lax.axis_index("state")
    own = width // layers
    slot_dev = k_tiles.shape[1]
    device = lax.axis_index(("row", "col"))
    span = rows_blk + 2 * REACH

    count = lax.axis_size(("row", "col"))
    forward = [(i, i + 1) for i in range(count - 1)]
    backward = [(b, a) for a, b in forward]
    low = lax.ppermute(vectors[rows_blk - REACH :], ("row", "col"), forward)
    high = lax.ppermute(vectors[:REACH], ("row", "col"), backward)

    tiles = jnp.stack([k_tiles, s_tiles]).reshape(2, rows_blk, slot_dev, layers, own, width)
    tiles = jnp.transpose(tiles, (3, 0, 1, 2, 4, 5))
    tiles = lax.all_to_all(tiles, "state", 0, 0, tiled=True)

    slot_ids = lax.broadcasted_iota(jnp.int32, columns.shape, 1)
    place = jnp.where(slot_ids < counts[:, None], columns - (device * rows_blk - REACH), span)
    place = jnp.clip(place, 0, span)
    diagonal = jnp.broadcast_to(onsite[:, :, None], (rows_blk, own, width))

    inner = lax.axis_size(("row", "state"))
    outer = lax.axis_size("col")
    outs = jax.ShapeDtypeStruct((rows_blk, states, own, width), jnp.float32)
    params = pltpu.CompilerParams(vmem_limit_bytes=LIMIT)
    kx, sx, stat = pl.pallas_call(
        functools.partial(product_kernel, states),
        out_shape=(outs, outs, jax.ShapeDtypeStruct((inner, 1, width), jnp.float32)),
        in_specs=[SMEM, SMEM] + [VMEM] * 5,
        out_specs=(VMEM, VMEM, VMEM),
        scratch_shapes=[pltpu.VMEM((2 * rows_blk * own, (span + 1) * width), jnp.bfloat16)],
        compiler_params=params,
    )(place, layer.reshape(1), tiles, low, vectors, high, diagonal)

    stat = lax.all_to_all(stat, ("row", "state"), 0, 0, tiled=True)
    stat = pl.pallas_call(
        functools.partial(merge_kernel, states),
        out_shape=jax.ShapeDtypeStruct((outer, 1, width), jnp.float32),
        in_specs=[VMEM],
        out_specs=VMEM,
    )(stat)
    stat = lax.all_to_all(stat, "col", 0, 0, tiled=True)
    correction, ritz = pl.pallas_call(
        functools.partial(final_kernel, states, count * rows_blk * width * width),
        out_shape=(outs, jax.ShapeDtypeStruct((1, width), jnp.float32)),
        in_specs=[VMEM] * 3,
        out_specs=(VMEM, VMEM),
    )(stat, kx, sx)
    return correction, ritz[0, :states]


def solution(mesh):
    placed = (
        P(("row", "col"), None, None, None),
        P(("row", "col"), "state"),
        P(("row", "col"), "state", None, None),
        P(("row", "col"), "state", None, None),
        P(("row", "col"), None),
        P(("row", "col")),
    )
    return jax.shard_map(
        per_device,
        mesh=mesh,
        in_specs=placed,
        out_specs=(P(("row", "col"), None, "state", None), P()),
        check_vma=False,
    )
```

```python
import functools

import jax
import jax.numpy as jnp
from jax import lax
from jax.experimental import pallas as pl
from jax.experimental.pallas import tpu as pltpu
from jax.sharding import PartitionSpec as P

REACH = 8
EPS = 1e-06
MIB = 1024 * 1024
VMEM = pl.BlockSpec(memory_space=pltpu.VMEM)
SMEM = pl.BlockSpec(memory_space=pltpu.SMEM)
ANY = pl.BlockSpec(memory_space=pl.ANY)


def limit(mib):
    return pltpu.CompilerParams(vmem_limit_bytes=mib * MIB)


def lanes(values, width=128):
    lane = lax.broadcasted_iota(jnp.int32, (1, width), 1)
    row = jnp.zeros((1, width), jnp.float32)
    for k, value in enumerate(values):
        row = jnp.where(lane == k, value, row)
    return row


def send_kernel(k_ref, s_ref, out_ref, held_ref, in_sems, out_sems):
    layers, _, _, _, own, _ = out_ref.shape
    pairs = [(d, op) for d in range(layers) for op in range(2)]
    loads = []
    for d, op in pairs:
        part = (k_ref, s_ref)[op].at[:, :, pl.ds(d * own, own), :]
        loads.append(pltpu.make_async_copy(part, held_ref.at[d, op], in_sems.at[d, op]))
        loads[-1].start()
    stores = []
    for (d, op), load in zip(pairs, loads):
        load.wait()
        stores.append(
            pltpu.make_async_copy(held_ref.at[d, op], out_ref.at[d, op], out_sems.at[d, op])
        )
        stores[-1].start()
    for store in stores:
        store.wait()


def merged(power, cross, norm):
    power_all = jnp.sum(power, axis=0, keepdims=True)
    cross_all = jnp.sum(cross, axis=0, keepdims=True)
    ratio = cross / (power + EPS)
    ritz = cross_all / (power_all + EPS)
    gap = ratio - ritz
    norm_all = jnp.sum(norm + (2 * EPS) * gap * ratio + gap * gap * power, axis=0, keepdims=True)
    return power_all, cross_all, norm_all, ritz


def merged_rows(parts, states):
    width = parts.shape[1]
    cross = pltpu.roll(parts, width - states, 1)
    norm = pltpu.roll(parts, width - 2 * states, 1)
    return merged(parts, cross, norm)


def pick(row, k):
    return row[:, k : k + 1]


def packed(power, cross, norm, states):
    return lanes([pick(a, k) for a in (power, cross, norm) for k in range(states)])


def early_kernel(
    states, spot_ref, columns_ref, counts_ref, tiles_ref, low_ref, mid_ref, onsite_ref, total_ref, oper_ref
):
    layers, _, rows, slot_dev, own, width = tiles_ref.shape
    half = rows * own
    window = oper_ref.shape[1] // width - 1
    oper_ref[:, : window * width] = jnp.zeros((2 * half, window * width), oper_ref.dtype)
    for i in range(rows):
        for y in range(layers):
            for m in range(slot_dev):
                slot = y * slot_dev + m
                block = columns_ref[i, slot] - spot_ref[0]
                block = jnp.where(slot < counts_ref[i], block, window)
                block = jnp.clip(block, 0, window)
                at = pl.ds(pl.multiple_of(block * width, width), width)
                for op in range(2):
                    top = op * half + i * own
                    oper_ref[top : top + own, at] = tiles_ref[y, op, i, m]

    square = (own, own)
    eye = lax.broadcasted_iota(jnp.int32, square, 0) == lax.broadcasted_iota(jnp.int32, square, 1)
    diagonal = []
    for i in range(rows):
        terms = jnp.where(eye, jnp.broadcast_to(onsite_ref[i : i + 1, :], square), 0.0)
        diagonal.append(jnp.broadcast_to(jnp.sum(terms, axis=1, keepdims=True), (own, width)))
    diagonal = jnp.concatenate(diagonal, axis=0)
    mine_at = pl.ds(pl.multiple_of(spot_ref[1] * own, own), own)
    for s in range(0, states, 2):
        mine = jnp.concatenate(
            [mid_ref[:, t, mine_at, :].astype(jnp.float32).reshape(half, width) for t in (s, s + 1)],
            axis=1,
        )
        both = jnp.concatenate([diagonal, diagonal], axis=1)
        total = jnp.concatenate([both * mine, mine], axis=0)
        at = 0
        for ref in (low_ref, mid_ref):
            total = total + product(oper_ref, at, ref, s)
            at += ref.shape[0] * width
        total_ref[:, s * width : (s + 2) * width] = total


def product(oper_ref, at, blocks_ref, s):
    width = blocks_ref.shape[-1]
    depth = blocks_ref.shape[0] * width
    blocks = jnp.concatenate(
        [blocks_ref[:, t].reshape(depth, width) for t in (s, s + 1)], axis=1
    )
    return jnp.dot(oper_ref[:, at : at + depth], blocks, preferred_element_type=jnp.float32)


def late_kernel(states, total_ref, oper_ref, high_ref, kx_ref, sx_ref, stat_ref):
    rows, _, own, width = kx_ref.shape
    half = rows * own
    at = oper_ref.shape[1] - (high_ref.shape[0] + 1) * width
    power, cross, norm = [], [], []
    for s in range(0, states, 2):
        total = total_ref[:, s * width : (s + 2) * width] + product(oper_ref, at, high_ref, s)
        for t in range(2):
            kx = total[:half, t * width : (t + 1) * width]
            sx = total[half:, t * width : (t + 1) * width]
            kx_ref[:, s + t] = kx.reshape(rows, own, width)
            sx_ref[:, s + t] = sx.reshape(rows, own, width)
            p = jnp.sum(sx * sx, keepdims=True)
            c = jnp.sum(sx * kx, keepdims=True)
            resid = kx - (c / (p + EPS)) * sx
            power.append(p)
            cross.append(c)
            norm.append(jnp.sum(resid * resid, keepdims=True))
    row = lanes(power + cross + norm)
    stat_ref[...] = jnp.broadcast_to(row[None], stat_ref.shape)


def merge_kernel(states, parts_ref, stat_ref):
    power, cross, norm, _ = merged_rows(parts_ref[...].reshape(parts_ref.shape[0], -1), states)
    stat_ref[...] = jnp.broadcast_to(packed(power, cross, norm, states)[None], stat_ref.shape)


def final_kernel(states, cells, parts_ref, kx_ref, sx_ref, out_ref, ritz_ref):
    _, _, norm, ritz = merged_rows(parts_ref[...].reshape(parts_ref.shape[0], -1), states)
    scale = lax.rsqrt(norm / cells + EPS)
    for s in range(states):
        out_ref[:, s] = (kx_ref[:, s] - pick(ritz, s)[None] * sx_ref[:, s]) * pick(scale, s)[None]
        ritz_ref[s] = ritz[0, s]


def per_device(vectors, onsite, k_tiles, s_tiles, columns, counts):
    rows_blk, states, width, _ = vectors.shape
    layers = lax.axis_size("state")
    layer = lax.axis_index("state")
    own = width // layers
    slot_dev = k_tiles.shape[1]
    device = lax.axis_index(("row", "col"))
    window = rows_blk + 2 * REACH

    count = lax.axis_size(("row", "col"))
    forward = [(i, i + 1) for i in range(count - 1)]
    backward = [(b, a) for a, b in forward]
    low = lax.ppermute(vectors[rows_blk - REACH :], ("row", "col"), forward)
    high = lax.ppermute(vectors[:REACH], ("row", "col"), backward)

    send = pl.pallas_call(
        send_kernel,
        out_shape=jax.ShapeDtypeStruct((layers, 2, rows_blk, slot_dev, own, width), k_tiles.dtype),
        in_specs=[ANY, ANY],
        out_specs=ANY,
        scratch_shapes=[
            pltpu.VMEM((layers, 2, rows_blk, slot_dev, own, width), k_tiles.dtype),
            pltpu.SemaphoreType.DMA((layers, 2)),
            pltpu.SemaphoreType.DMA((layers, 2)),
        ],
        compiler_params=limit(8),
    )(*(pltpu.with_memory_space_constraint(t, pltpu.HBM) for t in (k_tiles, s_tiles)))
    tiles = lax.all_to_all(send, "state", 0, 0, tiled=True)

    spot = jnp.stack([device * rows_blk - REACH, layer])
    tall = 2 * rows_blk * own
    total, oper = pl.pallas_call(
        functools.partial(early_kernel, states),
        out_shape=(
            jax.ShapeDtypeStruct((tall, states * width), jnp.float32),
            jax.ShapeDtypeStruct((tall, (window + 1) * width), vectors.dtype),
        ),
        in_specs=[SMEM] * 3 + [VMEM] * 4,
        out_specs=(VMEM, VMEM),
        compiler_params=limit(12),
    )(spot, columns, counts, tiles, low, vectors, onsite)

    inner = lax.axis_size(("row", "state"))
    outer = lax.axis_size("col")
    outs = jax.ShapeDtypeStruct((rows_blk, states, own, width), jnp.float32)
    kx, sx, stat = pl.pallas_call(
        functools.partial(late_kernel, states),
        out_shape=(outs, outs, jax.ShapeDtypeStruct((inner, 1, width), jnp.float32)),
        in_specs=[VMEM] * 3,
        out_specs=(VMEM, VMEM, VMEM),
        compiler_params=limit(12),
    )(total, oper, high)

    stat = lax.all_to_all(stat, ("row", "state"), 0, 0, tiled=True)
    stat = pl.pallas_call(
        functools.partial(merge_kernel, states),
        out_shape=jax.ShapeDtypeStruct((outer, 1, width), jnp.float32),
        in_specs=[VMEM],
        out_specs=VMEM,
        compiler_params=limit(2),
    )(stat)
    stat = lax.all_to_all(stat, "col", 0, 0, tiled=True)
    correction, ritz = pl.pallas_call(
        functools.partial(final_kernel, states, count * rows_blk * width * width),
        out_shape=(outs, jax.ShapeDtypeStruct((states,), jnp.float32)),
        in_specs=[VMEM] * 3,
        out_specs=(VMEM, SMEM),
        compiler_params=limit(4),
    )(stat, kx, sx)
    return correction, ritz


def solution(mesh):
    placed = (
        P(("row", "col"), None, None, None),
        P(("row", "col"), "state"),
        P(("row", "col"), "state", None, None),
        P(("row", "col"), "state", None, None),
        P(("row", "col"), None),
        P(("row", "col")),
    )
    return jax.shard_map(
        per_device,
        mesh=mesh,
        in_specs=placed,
        out_specs=(P(("row", "col"), None, "state", None), P()),
        check_vma=False,
    )
```

```python
import functools

import jax
import jax.numpy as jnp
from jax import lax
from jax.experimental import pallas as pl
from jax.experimental.pallas import tpu as pltpu
from jax.sharding import PartitionSpec as P

REACH = 8
EPS = 1e-06
MIB = 1024 * 1024
VMEM = pl.BlockSpec(memory_space=pltpu.VMEM)
SMEM = pl.BlockSpec(memory_space=pltpu.SMEM)
ANY = pl.BlockSpec(memory_space=pl.ANY)


def limit(mib):
    return pltpu.CompilerParams(vmem_limit_bytes=mib * MIB)


def lanes(values, width=128):
    lane = lax.broadcasted_iota(jnp.int32, (1, width), 1)
    row = jnp.zeros((1, width), jnp.float32)
    for k, value in enumerate(values):
        row = jnp.where(lane == k, value, row)
    return row


def send_kernel(lead, k_ref, s_ref, out_ref, held_ref, in_sems, out_sems):
    layers, _, _, _, own, _ = out_ref.shape
    pairs = [(d, op) for d in range(layers) for op in range(2)]
    loads = []
    for d, op in pairs:
        top = (lead + d) % layers * own
        part = (k_ref, s_ref)[op].at[:, :, pl.ds(top, own), :]
        loads.append(pltpu.make_async_copy(part, held_ref.at[d, op], in_sems.at[d, op]))
        loads[-1].start()
    stores = []
    for (d, op), load in zip(pairs, loads):
        load.wait()
        stores.append(
            pltpu.make_async_copy(held_ref.at[d, op], out_ref.at[d, op], out_sems.at[d, op])
        )
        stores[-1].start()
    for store in stores:
        store.wait()


def merged(power, cross, norm):
    power_all = jnp.sum(power, axis=0, keepdims=True)
    cross_all = jnp.sum(cross, axis=0, keepdims=True)
    ratio = cross / (power + EPS)
    ritz = cross_all / (power_all + EPS)
    gap = ratio - ritz
    norm_all = jnp.sum(norm + (2 * EPS) * gap * ratio + gap * gap * power, axis=0, keepdims=True)
    return power_all, cross_all, norm_all, ritz


def merged_rows(parts, states):
    width = parts.shape[1]
    cross = pltpu.roll(parts, width - states, 1)
    norm = pltpu.roll(parts, width - 2 * states, 1)
    return merged(parts, cross, norm)


def pick(row, k):
    return row[:, k : k + 1]


def packed(power, cross, norm, states):
    return lanes([pick(a, k) for a in (power, cross, norm) for k in range(states)])


def early_kernel(
    states, lead, spot_ref, columns_ref, counts_ref, tiles_ref, low_ref, mid_ref, onsite_ref, total_ref, oper_ref
):
    layers, _, rows, slot_dev, own, width = tiles_ref.shape
    half = rows * own
    window = oper_ref.shape[1] // width - 1
    oper_ref[:, : window * width] = jnp.zeros((2 * half, window * width), oper_ref.dtype)
    for i in range(rows):
        for y in range(layers):
            for m in range(slot_dev):
                slot = (lead + y) % layers * slot_dev + m
                block = columns_ref[i, slot] - spot_ref[0]
                block = jnp.where(slot < counts_ref[i], block, window)
                block = jnp.clip(block, 0, window)
                at = pl.ds(pl.multiple_of(block * width, width), width)
                for op in range(2):
                    top = op * half + i * own
                    oper_ref[top : top + own, at] = tiles_ref[y, op, i, m]

    square = (own, own)
    eye = lax.broadcasted_iota(jnp.int32, square, 0) == lax.broadcasted_iota(jnp.int32, square, 1)
    diagonal = []
    for i in range(rows):
        terms = jnp.where(eye, jnp.broadcast_to(onsite_ref[i : i + 1, :], square), 0.0)
        diagonal.append(jnp.broadcast_to(jnp.sum(terms, axis=1, keepdims=True), (own, width)))
    diagonal = jnp.concatenate(diagonal, axis=0)
    mine_at = pl.ds(pl.multiple_of(spot_ref[1] * own, own), own)
    for s in range(0, states, 2):
        mine = jnp.concatenate(
            [mid_ref[:, t, mine_at, :].astype(jnp.float32).reshape(half, width) for t in (s, s + 1)],
            axis=1,
        )
        both = jnp.concatenate([diagonal, diagonal], axis=1)
        total = jnp.concatenate([both * mine, mine], axis=0)
        at = 0
        for ref in (low_ref, mid_ref):
            total = total + product(oper_ref, at, ref, s)
            at += ref.shape[0] * width
        total_ref[:, s * width : (s + 2) * width] = total


def product(oper_ref, at, blocks_ref, s):
    width = blocks_ref.shape[-1]
    depth = blocks_ref.shape[0] * width
    blocks = jnp.concatenate(
        [blocks_ref[:, t].reshape(depth, width) for t in (s, s + 1)], axis=1
    )
    return jnp.dot(oper_ref[:, at : at + depth], blocks, preferred_element_type=jnp.float32)


def late_kernel(states, total_ref, oper_ref, high_ref, kx_ref, sx_ref, stat_ref):
    rows, _, own, width = kx_ref.shape
    half = rows * own
    at = oper_ref.shape[1] - (high_ref.shape[0] + 1) * width
    power, cross, norm = [], [], []
    for s in range(0, states, 2):
        total = total_ref[:, s * width : (s + 2) * width] + product(oper_ref, at, high_ref, s)
        for t in range(2):
            kx = total[:half, t * width : (t + 1) * width]
            sx = total[half:, t * width : (t + 1) * width]
            kx_ref[:, s + t] = kx.reshape(rows, own, width)
            sx_ref[:, s + t] = sx.reshape(rows, own, width)
            p = jnp.sum(sx * sx, keepdims=True)
            c = jnp.sum(sx * kx, keepdims=True)
            resid = kx - (c / (p + EPS)) * sx
            power.append(p)
            cross.append(c)
            norm.append(jnp.sum(resid * resid, keepdims=True))
    row = lanes(power + cross + norm)
    stat_ref[...] = jnp.broadcast_to(row[None], stat_ref.shape)


def merge_kernel(states, parts_ref, stat_ref):
    power, cross, norm, _ = merged_rows(parts_ref[...].reshape(parts_ref.shape[0], -1), states)
    stat_ref[...] = jnp.broadcast_to(packed(power, cross, norm, states)[None], stat_ref.shape)


def final_kernel(states, cells, parts_ref, kx_ref, sx_ref, out_ref, ritz_ref):
    _, _, norm, ritz = merged_rows(parts_ref[...].reshape(parts_ref.shape[0], -1), states)
    scale = lax.rsqrt(norm / cells + EPS)
    for s in range(states):
        out_ref[:, s] = (kx_ref[:, s] - pick(ritz, s)[None] * sx_ref[:, s]) * pick(scale, s)[None]
        ritz_ref[s] = ritz[0, s]


def ring_from(lead, size):
    return [[(lead + k) % size for k in range(size)]]


def per_device(vectors, onsite, k_tiles, s_tiles, columns, counts):
    rows_blk, states, width, _ = vectors.shape
    layers = lax.axis_size("state")
    layer = lax.axis_index("state")
    own = width // layers
    slot_dev = k_tiles.shape[1]
    device = lax.axis_index(("row", "col"))
    window = rows_blk + 2 * REACH

    count = lax.axis_size(("row", "col"))
    forward = [(i, i + 1) for i in range(count - 1)]
    backward = [(b, a) for a, b in forward]
    low = lax.ppermute(vectors[rows_blk - REACH :], ("row", "col"), forward)
    high = lax.ppermute(vectors[:REACH], ("row", "col"), backward)

    lead = layers // 2
    send = pl.pallas_call(
        functools.partial(send_kernel, lead),
        out_shape=jax.ShapeDtypeStruct((layers, 2, rows_blk, slot_dev, own, width), k_tiles.dtype),
        in_specs=[ANY, ANY],
        out_specs=ANY,
        scratch_shapes=[
            pltpu.VMEM((layers, 2, rows_blk, slot_dev, own, width), k_tiles.dtype),
            pltpu.SemaphoreType.DMA((layers, 2)),
            pltpu.SemaphoreType.DMA((layers, 2)),
        ],
        compiler_params=limit(8),
    )(*(pltpu.with_memory_space_constraint(t, pltpu.HBM) for t in (k_tiles, s_tiles)))
    tiles = lax.all_to_all(
        send, "state", 0, 0, axis_index_groups=ring_from(lead, layers), tiled=True
    )

    spot = jnp.stack([device * rows_blk - REACH, layer])
    tall = 2 * rows_blk * own
    total, oper = pl.pallas_call(
        functools.partial(early_kernel, states, lead),
        out_shape=(
            jax.ShapeDtypeStruct((tall, states * width), jnp.float32),
            jax.ShapeDtypeStruct((tall, (window + 1) * width), vectors.dtype),
        ),
        in_specs=[SMEM] * 3 + [VMEM] * 4,
        out_specs=(VMEM, VMEM),
        compiler_params=limit(12),
    )(spot, columns, counts, tiles, low, vectors, onsite)

    inner = lax.axis_size(("row", "state"))
    outer = lax.axis_size("col")
    late_plane = inner - 2 * layers + lead
    late_col = outer // 2 + 1
    outs = jax.ShapeDtypeStruct((rows_blk, states, own, width), jnp.float32)
    kx, sx, stat = pl.pallas_call(
        functools.partial(late_kernel, states),
        out_shape=(outs, outs, jax.ShapeDtypeStruct((inner, 1, width), jnp.float32)),
        in_specs=[VMEM] * 3,
        out_specs=(VMEM, VMEM, VMEM),
        compiler_params=limit(12),
    )(total, oper, high)

    stat = lax.all_to_all(
        stat, ("row", "state"), 0, 0, axis_index_groups=ring_from(late_plane, inner), tiled=True
    )
    stat = pl.pallas_call(
        functools.partial(merge_kernel, states),
        out_shape=jax.ShapeDtypeStruct((outer, 1, width), jnp.float32),
        in_specs=[VMEM],
        out_specs=VMEM,
        compiler_params=limit(2),
    )(stat)
    stat = lax.all_to_all(
        stat, "col", 0, 0, axis_index_groups=ring_from(late_col, outer), tiled=True
    )
    correction, ritz = pl.pallas_call(
        functools.partial(final_kernel, states, count * rows_blk * width * width),
        out_shape=(outs, jax.ShapeDtypeStruct((states,), jnp.float32)),
        in_specs=[VMEM] * 3,
        out_specs=(VMEM, SMEM),
        compiler_params=limit(4),
    )(stat, kx, sx)
    return correction, ritz


def solution(mesh):
    placed = (
        P(("row", "col"), None, None, None),
        P(("row", "col"), "state"),
        P(("row", "col"), "state", None, None),
        P(("row", "col"), "state", None, None),
        P(("row", "col"), None),
        P(("row", "col")),
    )
    return jax.shard_map(
        per_device,
        mesh=mesh,
        in_specs=placed,
        out_specs=(P(("row", "col"), None, "state", None), P()),
        check_vma=False,
    )
```

```python
import functools

import jax
import jax.numpy as jnp
from jax import lax
from jax.experimental import pallas as pl
from jax.experimental.pallas import tpu as pltpu
from jax.sharding import PartitionSpec as P

REACH = 8
EPS = 1e-06
MIB = 1024 * 1024
VMEM = pl.BlockSpec(memory_space=pltpu.VMEM)
SMEM = pl.BlockSpec(memory_space=pltpu.SMEM)
ANY = pl.BlockSpec(memory_space=pl.ANY)


def limit(mib):
    return pltpu.CompilerParams(vmem_limit_bytes=mib * MIB)


def lanes(values, width=128):
    lane = lax.broadcasted_iota(jnp.int32, (1, width), 1)
    row = jnp.zeros((1, width), jnp.float32)
    for k, value in enumerate(values):
        row = jnp.where(lane == k, value, row)
    return row


def send_kernel(order, k_ref, s_ref, out_ref, held_ref, in_sems, out_sems):
    layers, _, _, _, own, _ = out_ref.shape
    pairs = [(d, op) for d in range(layers) for op in range(2)]
    loads = []
    for d, op in pairs:
        top = order[d] * own
        part = (k_ref, s_ref)[op].at[:, :, pl.ds(top, own), :]
        loads.append(pltpu.make_async_copy(part, held_ref.at[d, op], in_sems.at[d, op]))
        loads[-1].start()
    stores = []
    for (d, op), load in zip(pairs, loads):
        load.wait()
        stores.append(
            pltpu.make_async_copy(held_ref.at[d, op], out_ref.at[d, op], out_sems.at[d, op])
        )
        stores[-1].start()
    for store in stores:
        store.wait()


def merged(power, cross, norm):
    power_all = jnp.sum(power, axis=0, keepdims=True)
    cross_all = jnp.sum(cross, axis=0, keepdims=True)
    ratio = cross / (power + EPS)
    ritz = cross_all / (power_all + EPS)
    gap = ratio - ritz
    norm_all = jnp.sum(norm + (2 * EPS) * gap * ratio + gap * gap * power, axis=0, keepdims=True)
    return power_all, cross_all, norm_all, ritz


def merged_rows(parts, states):
    width = parts.shape[1]
    cross = pltpu.roll(parts, width - states, 1)
    norm = pltpu.roll(parts, width - 2 * states, 1)
    return merged(parts, cross, norm)


def pick(row, k):
    return row[:, k : k + 1]


def packed(power, cross, norm, states):
    return lanes([pick(a, k) for a in (power, cross, norm) for k in range(states)])


def early_kernel(
    states, order, spot_ref, columns_ref, counts_ref, tiles_ref, low_ref, mid_ref, onsite_ref, total_ref, oper_ref
):
    layers, _, rows, slot_dev, own, width = tiles_ref.shape
    half = rows * own
    window = oper_ref.shape[1] // width - 1
    oper_ref[:, : window * width] = jnp.zeros((2 * half, window * width), oper_ref.dtype)
    for i in range(rows):
        for y in range(layers):
            for m in range(slot_dev):
                slot = order[y] * slot_dev + m
                block = columns_ref[i, slot] - spot_ref[0]
                block = jnp.where(slot < counts_ref[i], block, window)
                block = jnp.clip(block, 0, window)
                at = pl.ds(pl.multiple_of(block * width, width), width)
                for op in range(2):
                    top = op * half + i * own
                    oper_ref[top : top + own, at] = tiles_ref[y, op, i, m]

    square = (own, own)
    eye = lax.broadcasted_iota(jnp.int32, square, 0) == lax.broadcasted_iota(jnp.int32, square, 1)
    diagonal = []
    for i in range(rows):
        terms = jnp.where(eye, jnp.broadcast_to(onsite_ref[i : i + 1, :], square), 0.0)
        diagonal.append(jnp.broadcast_to(jnp.sum(terms, axis=1, keepdims=True), (own, width)))
    diagonal = jnp.concatenate(diagonal, axis=0)
    mine_at = pl.ds(pl.multiple_of(spot_ref[1] * own, own), own)
    for s in range(0, states, 2):
        mine = jnp.concatenate(
            [mid_ref[:, t, mine_at, :].astype(jnp.float32).reshape(half, width) for t in (s, s + 1)],
            axis=1,
        )
        both = jnp.concatenate([diagonal, diagonal], axis=1)
        total = jnp.concatenate([both * mine, mine], axis=0)
        at = 0
        for ref in (low_ref, mid_ref):
            total = total + product(oper_ref, at, ref, s)
            at += ref.shape[0] * width
        total_ref[:, s * width : (s + 2) * width] = total


def product(oper_ref, at, blocks_ref, s):
    width = blocks_ref.shape[-1]
    depth = blocks_ref.shape[0] * width
    blocks = jnp.concatenate(
        [blocks_ref[:, t].reshape(depth, width) for t in (s, s + 1)], axis=1
    )
    return jnp.dot(oper_ref[:, at : at + depth], blocks, preferred_element_type=jnp.float32)


def late_kernel(states, total_ref, oper_ref, high_ref, kx_ref, sx_ref, stat_ref):
    rows, _, own, width = kx_ref.shape
    half = rows * own
    at = oper_ref.shape[1] - (high_ref.shape[0] + 1) * width
    power, cross, norm = [], [], []
    for s in range(0, states, 2):
        total = total_ref[:, s * width : (s + 2) * width] + product(oper_ref, at, high_ref, s)
        for t in range(2):
            kx = total[:half, t * width : (t + 1) * width]
            sx = total[half:, t * width : (t + 1) * width]
            kx_ref[:, s + t] = kx.reshape(rows, own, width)
            sx_ref[:, s + t] = sx.reshape(rows, own, width)
            power.append(jnp.sum(sx * sx, axis=0, keepdims=True))
            cross.append(jnp.sum(sx * kx, axis=0, keepdims=True))
    sums = jnp.sum(jnp.concatenate(power + cross, axis=0), axis=1, keepdims=True)
    ratio = sums[states:] / (sums[:states] + EPS)
    for s in range(states):
        resid = kx_ref[:, s] - ratio[s : s + 1][None] * sx_ref[:, s]
        resid = resid.reshape(half, width)
        norm.append(jnp.sum(resid * resid, axis=0, keepdims=True))
    norm = jnp.sum(jnp.concatenate(norm, axis=0), axis=1, keepdims=True)
    column = jnp.concatenate([sums, norm], axis=0)
    shape = (3 * states, width)
    mine = lax.broadcasted_iota(jnp.int32, shape, 0) == lax.broadcasted_iota(jnp.int32, shape, 1)
    row = jnp.sum(jnp.where(mine, jnp.broadcast_to(column, shape), 0.0), axis=0, keepdims=True)
    stat_ref[...] = jnp.broadcast_to(row[None], stat_ref.shape)


def merge_kernel(states, parts_ref, stat_ref):
    power, cross, norm, _ = merged_rows(parts_ref[...].reshape(parts_ref.shape[0], -1), states)
    stat_ref[...] = jnp.broadcast_to(packed(power, cross, norm, states)[None], stat_ref.shape)


def final_kernel(states, cells, parts_ref, kx_ref, sx_ref, out_ref, ritz_ref):
    _, _, norm, ritz = merged_rows(parts_ref[...].reshape(parts_ref.shape[0], -1), states)
    scale = lax.rsqrt(norm / cells + EPS)
    for s in range(states):
        out_ref[:, s] = (kx_ref[:, s] - pick(ritz, s)[None] * sx_ref[:, s]) * pick(scale, s)[None]
        ritz_ref[s] = ritz[0, s]


def led(group, lead):
    return [lead] + [m for m in group if m != lead]


def sum_phases(rows, cols, layers):
    lines = [
        led([row * cols + c for row in (x, x + 1) for c in range(cols)], x * cols + cols // 2 + 1)
        for x in range(0, rows, 2)
    ]
    planes = [
        led(
            [row * layers + m for row in range(core, rows, 2) for m in range(layers)],
            (rows - 2 + core) * layers + layers // 2,
        )
        for core in range(2)
    ]
    return [(("row", "col"), lines), (("row", "state"), planes)]


def per_device(vectors, onsite, k_tiles, s_tiles, columns, counts):
    rows_blk, states, width, _ = vectors.shape
    layers = lax.axis_size("state")
    layer = lax.axis_index("state")
    own = width // layers
    slot_dev = k_tiles.shape[1]
    device = lax.axis_index(("row", "col"))
    window = rows_blk + 2 * REACH

    count = lax.axis_size(("row", "col"))
    forward = [(i, i + 1) for i in range(count - 1)]
    backward = [(b, a) for a, b in forward]
    low = lax.ppermute(vectors[rows_blk - REACH :], ("row", "col"), forward)
    high = lax.ppermute(vectors[:REACH], ("row", "col"), backward)

    half = layers // 2
    order = [k // 2 + (half if k % 2 == 0 else 0) for k in range(layers)]
    send = pl.pallas_call(
        functools.partial(send_kernel, order),
        out_shape=jax.ShapeDtypeStruct((layers, 2, rows_blk, slot_dev, own, width), k_tiles.dtype),
        in_specs=[ANY, ANY],
        out_specs=ANY,
        scratch_shapes=[
            pltpu.VMEM((layers, 2, rows_blk, slot_dev, own, width), k_tiles.dtype),
            pltpu.SemaphoreType.DMA((layers, 2)),
            pltpu.SemaphoreType.DMA((layers, 2)),
        ],
        compiler_params=limit(8),
    )(*(pltpu.with_memory_space_constraint(t, pltpu.HBM) for t in (k_tiles, s_tiles)))
    tiles = lax.all_to_all(
        send, "state", 0, 0, axis_index_groups=[order], tiled=True
    )

    spot = jnp.stack([device * rows_blk - REACH, layer])
    tall = 2 * rows_blk * own
    total, oper = pl.pallas_call(
        functools.partial(early_kernel, states, order),
        out_shape=(
            jax.ShapeDtypeStruct((tall, states * width), jnp.float32),
            jax.ShapeDtypeStruct((tall, (window + 1) * width), vectors.dtype),
        ),
        in_specs=[SMEM] * 3 + [VMEM] * 4,
        out_specs=(VMEM, VMEM),
        compiler_params=limit(12),
    )(spot, columns, counts, tiles, low, vectors, onsite)

    phases = sum_phases(lax.axis_size("row"), lax.axis_size("col"), layers)
    inner, outer = (len(groups[0]) for _, groups in phases)
    outs = jax.ShapeDtypeStruct((rows_blk, states, own, width), jnp.float32)
    kx, sx, stat = pl.pallas_call(
        functools.partial(late_kernel, states),
        out_shape=(outs, outs, jax.ShapeDtypeStruct((inner, 1, width), jnp.float32)),
        in_specs=[VMEM] * 3,
        out_specs=(VMEM, VMEM, VMEM),
        compiler_params=limit(12),
    )(total, oper, high)

    axes, groups = phases[0]
    stat = lax.all_to_all(stat, axes, 0, 0, axis_index_groups=groups, tiled=True)
    stat = pl.pallas_call(
        functools.partial(merge_kernel, states),
        out_shape=jax.ShapeDtypeStruct((outer, 1, width), jnp.float32),
        in_specs=[VMEM],
        out_specs=VMEM,
        compiler_params=limit(2),
    )(stat)
    axes, groups = phases[1]
    stat = lax.all_to_all(stat, axes, 0, 0, axis_index_groups=groups, tiled=True)
    correction, ritz = pl.pallas_call(
        functools.partial(final_kernel, states, count * rows_blk * width * width),
        out_shape=(outs, jax.ShapeDtypeStruct((states,), jnp.float32)),
        in_specs=[VMEM] * 3,
        out_specs=(VMEM, SMEM),
        compiler_params=limit(4),
    )(stat, kx, sx)
    return correction, ritz


def solution(mesh):
    placed = (
        P(("row", "col"), None, None, None),
        P(("row", "col"), "state"),
        P(("row", "col"), "state", None, None),
        P(("row", "col"), "state", None, None),
        P(("row", "col"), None),
        P(("row", "col")),
    )
    return jax.shard_map(
        per_device,
        mesh=mesh,
        in_specs=placed,
        out_specs=(P(("row", "col"), None, "state", None), P()),
        check_vma=False,
    )
```

```python
import functools

import jax
import jax.numpy as jnp
from jax import lax
from jax.experimental import pallas as pl
from jax.experimental.pallas import tpu as pltpu
from jax.sharding import PartitionSpec as P

REACH = 8
EPS = 1e-06
MIB = 1024 * 1024
VMEM = pl.BlockSpec(memory_space=pltpu.VMEM)
SMEM = pl.BlockSpec(memory_space=pltpu.SMEM)
ANY = pl.BlockSpec(memory_space=pl.ANY)


def limit(mib):
    return pltpu.CompilerParams(vmem_limit_bytes=mib * MIB)


def lanes(values, width=128):
    lane = lax.broadcasted_iota(jnp.int32, (1, width), 1)
    row = jnp.zeros((1, width), jnp.float32)
    for k, value in enumerate(values):
        row = jnp.where(lane == k, value, row)
    return row


def send_kernel(order, k_ref, s_ref, out_ref, held_ref, in_sems, out_sems):
    layers, _, _, _, own, _ = out_ref.shape
    pairs = [(d, op) for d in range(layers) for op in range(2)]
    loads = []
    for d, op in pairs:
        top = order[d] * own
        part = (k_ref, s_ref)[op].at[:, :, pl.ds(top, own), :]
        loads.append(pltpu.make_async_copy(part, held_ref.at[d, op], in_sems.at[d, op]))
        loads[-1].start()
    stores = []
    for (d, op), load in zip(pairs, loads):
        load.wait()
        stores.append(
            pltpu.make_async_copy(held_ref.at[d, op], out_ref.at[d, op], out_sems.at[d, op])
        )
        stores[-1].start()
    for store in stores:
        store.wait()


def merged(power, cross, norm):
    power_all = jnp.sum(power, axis=0, keepdims=True)
    cross_all = jnp.sum(cross, axis=0, keepdims=True)
    ratio = cross / (power + EPS)
    ritz = cross_all / (power_all + EPS)
    gap = ratio - ritz
    norm_all = jnp.sum(norm + (2 * EPS) * gap * ratio + gap * gap * power, axis=0, keepdims=True)
    return power_all, cross_all, norm_all, ritz


def merged_rows(parts, states):
    width = parts.shape[1]
    cross = pltpu.roll(parts, width - states, 1)
    norm = pltpu.roll(parts, width - 2 * states, 1)
    return merged(parts, cross, norm)


def pick(row, k):
    return row[:, k : k + 1]


def packed(power, cross, norm, states):
    return lanes([pick(a, k) for a in (power, cross, norm) for k in range(states)])


def early_kernel(
    states, order, spot_ref, columns_ref, counts_ref, tiles_ref, low_ref, mid_ref, onsite_ref, total_ref, oper_ref
):
    layers, _, rows, slot_dev, own, width = tiles_ref.shape
    half = rows * own
    window = oper_ref.shape[1] // width - 1
    oper_ref[:, : window * width] = jnp.zeros((2 * half, window * width), oper_ref.dtype)
    for i in range(rows):
        for y in range(layers):
            for m in range(slot_dev):
                slot = order[y] * slot_dev + m
                block = columns_ref[i, slot] - spot_ref[0]
                block = jnp.where(slot < counts_ref[i], block, window)
                block = jnp.clip(block, 0, window)
                at = pl.ds(pl.multiple_of(block * width, width), width)
                for op in range(2):
                    top = op * half + i * own
                    oper_ref[top : top + own, at] = tiles_ref[y, op, i, m]

    square = (own, own)
    eye = lax.broadcasted_iota(jnp.int32, square, 0) == lax.broadcasted_iota(jnp.int32, square, 1)
    diagonal = []
    for i in range(rows):
        terms = jnp.where(eye, jnp.broadcast_to(onsite_ref[i : i + 1, :], square), 0.0)
        diagonal.append(jnp.broadcast_to(jnp.sum(terms, axis=1, keepdims=True), (own, width)))
    diagonal = jnp.concatenate(diagonal, axis=0)
    mine_at = pl.ds(pl.multiple_of(spot_ref[1] * own, own), own)
    for s in range(0, states, 2):
        mine = jnp.concatenate(
            [mid_ref[:, t, mine_at, :].astype(jnp.float32).reshape(half, width) for t in (s, s + 1)],
            axis=1,
        )
        both = jnp.concatenate([diagonal, diagonal], axis=1)
        total = jnp.concatenate([both * mine, mine], axis=0)
        at = 0
        for ref in (low_ref, mid_ref):
            total = total + product(oper_ref, at, ref, s)
            at += ref.shape[0] * width
        total_ref[:, s * width : (s + 2) * width] = total


def product(oper_ref, at, blocks_ref, s):
    width = blocks_ref.shape[-1]
    depth = blocks_ref.shape[0] * width
    blocks = jnp.concatenate(
        [blocks_ref[:, t].reshape(depth, width) for t in (s, s + 1)], axis=1
    )
    return jnp.dot(oper_ref[:, at : at + depth], blocks, preferred_element_type=jnp.float32)


def late_kernel(states, total_ref, oper_ref, high_ref, kx_ref, sx_ref, stat_ref):
    rows, _, own, width = kx_ref.shape
    half = rows * own
    at = oper_ref.shape[1] - (high_ref.shape[0] + 1) * width
    power, cross, norm = [], [], []
    for s in range(0, states, 2):
        total = total_ref[:, s * width : (s + 2) * width] + product(oper_ref, at, high_ref, s)
        for t in range(2):
            kx = total[:half, t * width : (t + 1) * width]
            sx = total[half:, t * width : (t + 1) * width]
            kx_ref[:, s + t] = kx.reshape(rows, own, width)
            sx_ref[:, s + t] = sx.reshape(rows, own, width)
            power.append(jnp.sum(sx * sx, axis=0, keepdims=True))
            cross.append(jnp.sum(sx * kx, axis=0, keepdims=True))
    sums = jnp.sum(jnp.concatenate(power + cross, axis=0), axis=1, keepdims=True)
    ratio = sums[states:] / (sums[:states] + EPS)
    for s in range(states):
        resid = kx_ref[:, s] - ratio[s : s + 1][None] * sx_ref[:, s]
        resid = resid.reshape(half, width)
        norm.append(jnp.sum(resid * resid, axis=0, keepdims=True))
    norm = jnp.sum(jnp.concatenate(norm, axis=0), axis=1, keepdims=True)
    column = jnp.concatenate([sums, norm], axis=0)
    shape = (3 * states, width)
    mine = lax.broadcasted_iota(jnp.int32, shape, 0) == lax.broadcasted_iota(jnp.int32, shape, 1)
    row = jnp.sum(jnp.where(mine, jnp.broadcast_to(column, shape), 0.0), axis=0, keepdims=True)
    stat_ref[...] = jnp.broadcast_to(row[None], stat_ref.shape)


def merge_kernel(states, parts_ref, stat_ref):
    power, cross, norm, _ = merged_rows(parts_ref[...].reshape(parts_ref.shape[0], -1), states)
    stat_ref[...] = jnp.broadcast_to(packed(power, cross, norm, states)[None], stat_ref.shape)


def final_kernel(states, cells, parts_ref, kx_ref, sx_ref, out_ref, ritz_ref, held_ref, sems):
    _, _, norm, ritz = merged_rows(parts_ref[...].reshape(parts_ref.shape[0], -1), states)
    scale = lax.rsqrt(norm / cells + EPS)
    rows = held_ref.shape[0]
    part = rows // 2
    stores = []
    for n in range(2):
        here = pl.ds(n * part, part)
        for s in range(states):
            resid = kx_ref[here, s] - pick(ritz, s)[None] * sx_ref[here, s]
            held_ref[here, s] = resid * pick(scale, s)[None]
        stores.append(pltpu.make_async_copy(held_ref.at[here], out_ref.at[here], sems.at[n]))
        stores[-1].start()
    for s in range(states):
        ritz_ref[s] = ritz[0, s]
    for store in stores:
        store.wait()


def led(group, lead):
    return [lead] + [m for m in group if m != lead]


def sum_phases(rows, cols, layers):
    lines = [
        led([row * cols + c for row in (x, x + 1) for c in range(cols)], (x + 1) * cols + cols // 2 + 1)
        for x in range(0, rows, 2)
    ]
    planes = [
        led(
            [row * layers + m for row in range(core, rows, 2) for m in range(layers)],
            (rows - 2 + core) * layers + layers // 2,
        )
        for core in range(2)
    ]
    return [(("row", "col"), lines), (("row", "state"), planes)]


def per_device(vectors, onsite, k_tiles, s_tiles, columns, counts):
    rows_blk, states, width, _ = vectors.shape
    layers = lax.axis_size("state")
    layer = lax.axis_index("state")
    own = width // layers
    slot_dev = k_tiles.shape[1]
    device = lax.axis_index(("row", "col"))
    window = rows_blk + 2 * REACH

    count = lax.axis_size(("row", "col"))
    forward = [(i, i + 1) for i in range(count - 1)]
    backward = [(b, a) for a, b in forward]
    low = lax.ppermute(vectors[rows_blk - REACH :], ("row", "col"), forward)
    high = lax.ppermute(vectors[:REACH], ("row", "col"), backward)

    half = layers // 2
    order = [k // 2 + (half if k % 2 == 0 else 0) for k in range(layers)]
    send = pl.pallas_call(
        functools.partial(send_kernel, order),
        out_shape=jax.ShapeDtypeStruct((layers, 2, rows_blk, slot_dev, own, width), k_tiles.dtype),
        in_specs=[ANY, ANY],
        out_specs=ANY,
        scratch_shapes=[
            pltpu.VMEM((layers, 2, rows_blk, slot_dev, own, width), k_tiles.dtype),
            pltpu.SemaphoreType.DMA((layers, 2)),
            pltpu.SemaphoreType.DMA((layers, 2)),
        ],
        compiler_params=limit(8),
    )(*(pltpu.with_memory_space_constraint(t, pltpu.HBM) for t in (k_tiles, s_tiles)))
    tiles = lax.all_to_all(
        send, "state", 0, 0, axis_index_groups=[order], tiled=True
    )

    spot = jnp.stack([device * rows_blk - REACH, layer])
    tall = 2 * rows_blk * own
    total, oper = pl.pallas_call(
        functools.partial(early_kernel, states, order),
        out_shape=(
            jax.ShapeDtypeStruct((tall, states * width), jnp.float32),
            jax.ShapeDtypeStruct((tall, (window + 1) * width), vectors.dtype),
        ),
        in_specs=[SMEM] * 3 + [VMEM] * 4,
        out_specs=(VMEM, VMEM),
        compiler_params=limit(12),
    )(spot, columns, counts, tiles, low, vectors, onsite)

    phases = sum_phases(lax.axis_size("row"), lax.axis_size("col"), layers)
    inner, outer = (len(groups[0]) for _, groups in phases)
    outs = jax.ShapeDtypeStruct((rows_blk, states, own, width), jnp.float32)
    kx, sx, stat = pl.pallas_call(
        functools.partial(late_kernel, states),
        out_shape=(outs, outs, jax.ShapeDtypeStruct((inner, 1, width), jnp.float32)),
        in_specs=[VMEM] * 3,
        out_specs=(VMEM, VMEM, VMEM),
        compiler_params=limit(12),
    )(total, oper, high)

    axes, groups = phases[0]
    stat = lax.all_to_all(stat, axes, 0, 0, axis_index_groups=groups, tiled=True)
    stat = pl.pallas_call(
        functools.partial(merge_kernel, states),
        out_shape=jax.ShapeDtypeStruct((outer, 1, width), jnp.float32),
        in_specs=[VMEM],
        out_specs=VMEM,
        compiler_params=limit(2),
    )(stat)
    axes, groups = phases[1]
    stat = lax.all_to_all(stat, axes, 0, 0, axis_index_groups=groups, tiled=True)
    correction, ritz = pl.pallas_call(
        functools.partial(final_kernel, states, count * rows_blk * width * width),
        out_shape=(outs, jax.ShapeDtypeStruct((states,), jnp.float32)),
        in_specs=[VMEM] * 3,
        out_specs=(ANY, SMEM),
        scratch_shapes=[
            pltpu.VMEM((rows_blk, states, own, width), jnp.float32),
            pltpu.SemaphoreType.DMA((2,)),
        ],
        compiler_params=limit(4),
    )(stat, kx, sx)
    return correction, ritz


def solution(mesh):
    placed = (
        P(("row", "col"), None, None, None),
        P(("row", "col"), "state"),
        P(("row", "col"), "state", None, None),
        P(("row", "col"), "state", None, None),
        P(("row", "col"), None),
        P(("row", "col")),
    )
    return jax.shard_map(
        per_device,
        mesh=mesh,
        in_specs=placed,
        out_specs=(P(("row", "col"), None, "state", None), P()),
        check_vma=False,
    )
```

```python
import functools

import jax
import jax.numpy as jnp
from jax import lax
from jax.experimental import pallas as pl
from jax.experimental.pallas import tpu as pltpu
from jax.sharding import PartitionSpec as P

REACH = 8
EPS = 1e-06
MIB = 1024 * 1024
VMEM = pl.BlockSpec(memory_space=pltpu.VMEM)
SMEM = pl.BlockSpec(memory_space=pltpu.SMEM)
ANY = pl.BlockSpec(memory_space=pl.ANY)


def limit(mib):
    return pltpu.CompilerParams(vmem_limit_bytes=mib * MIB)


def lanes(values, width=128):
    lane = lax.broadcasted_iota(jnp.int32, (1, width), 1)
    row = jnp.zeros((1, width), jnp.float32)
    for k, value in enumerate(values):
        row = jnp.where(lane == k, value, row)
    return row


def send_kernel(order, k_ref, s_ref, out_ref, held_ref, in_sems, out_sems):
    layers, _, _, _, own, _ = out_ref.shape
    pairs = [(d, op) for d in range(layers) for op in range(2)]
    loads = []
    for d, op in pairs:
        top = order[d] * own
        part = (k_ref, s_ref)[op].at[:, :, pl.ds(top, own), :]
        loads.append(pltpu.make_async_copy(part, held_ref.at[d, op], in_sems.at[d, op]))
        loads[-1].start()
    stores = []
    for (d, op), load in zip(pairs, loads):
        load.wait()
        stores.append(
            pltpu.make_async_copy(held_ref.at[d, op], out_ref.at[d, op], out_sems.at[d, op])
        )
        stores[-1].start()
    for store in stores:
        store.wait()


def merged(power, cross, norm):
    power_all = jnp.sum(power, axis=0, keepdims=True)
    cross_all = jnp.sum(cross, axis=0, keepdims=True)
    ratio = cross / (power + EPS)
    ritz = cross_all / (power_all + EPS)
    gap = ratio - ritz
    norm_all = jnp.sum(norm + (2 * EPS) * gap * ratio + gap * gap * power, axis=0, keepdims=True)
    return power_all, cross_all, norm_all, ritz


def merged_rows(parts, states):
    width = parts.shape[1]
    cross = pltpu.roll(parts, width - states, 1)
    norm = pltpu.roll(parts, width - 2 * states, 1)
    return merged(parts, cross, norm)


def pick(row, k):
    return row[:, k : k + 1]


def packed(power, cross, norm, states):
    return lanes([pick(a, k) for a in (power, cross, norm) for k in range(states)])


def early_kernel(
    states, order, spot_ref, columns_ref, counts_ref, tiles_ref, low_ref, mid_ref, onsite_ref, total_ref, oper_ref
):
    layers, _, rows, slot_dev, own, width = tiles_ref.shape
    half = rows * own
    window = oper_ref.shape[1] // width - 1
    oper_ref[:, : window * width] = jnp.zeros((2 * half, window * width), oper_ref.dtype)
    for i in range(rows):
        for y in range(layers):
            for m in range(slot_dev):
                slot = order[y] * slot_dev + m
                block = columns_ref[i, slot] - spot_ref[0]
                block = jnp.where(slot < counts_ref[i], block, window)
                block = jnp.clip(block, 0, window)
                at = pl.ds(pl.multiple_of(block * width, width), width)
                for op in range(2):
                    top = op * half + i * own
                    oper_ref[top : top + own, at] = tiles_ref[y, op, i, m]

    square = (own, own)
    eye = lax.broadcasted_iota(jnp.int32, square, 0) == lax.broadcasted_iota(jnp.int32, square, 1)
    diagonal = []
    for i in range(rows):
        terms = jnp.where(eye, jnp.broadcast_to(onsite_ref[i : i + 1, :], square), 0.0)
        diagonal.append(jnp.broadcast_to(jnp.sum(terms, axis=1, keepdims=True), (own, width)))
    diagonal = jnp.concatenate(diagonal, axis=0)
    mine_at = pl.ds(pl.multiple_of(spot_ref[1] * own, own), own)
    for s in range(0, states, 2):
        mine = jnp.concatenate(
            [mid_ref[:, t, mine_at, :].astype(jnp.float32).reshape(half, width) for t in (s, s + 1)],
            axis=1,
        )
        both = jnp.concatenate([diagonal, diagonal], axis=1)
        total = jnp.concatenate([both * mine, mine], axis=0)
        at = 0
        for ref in (low_ref, mid_ref):
            total = total + product(oper_ref, at, ref, s)
            at += ref.shape[0] * width
        total_ref[:, s * width : (s + 2) * width] = total


def product(oper_ref, at, blocks_ref, s):
    width = blocks_ref.shape[-1]
    depth = blocks_ref.shape[0] * width
    blocks = jnp.concatenate(
        [blocks_ref[:, t].reshape(depth, width) for t in (s, s + 1)], axis=1
    )
    return jnp.dot(oper_ref[:, at : at + depth], blocks, preferred_element_type=jnp.float32)


def late_kernel(states, total_ref, oper_ref, high_ref, kx_ref, sx_ref, stat_ref):
    rows, _, own, width = kx_ref.shape
    half = rows * own
    at = oper_ref.shape[1] - (high_ref.shape[0] + 1) * width
    power, cross, norm = [], [], []
    for s in range(0, states, 2):
        total = total_ref[:, s * width : (s + 2) * width] + product(oper_ref, at, high_ref, s)
        for t in range(2):
            kx = total[:half, t * width : (t + 1) * width]
            sx = total[half:, t * width : (t + 1) * width]
            kx_ref[:, s + t] = kx.reshape(rows, own, width)
            sx_ref[:, s + t] = sx.reshape(rows, own, width)
            power.append(jnp.sum(sx * sx, axis=0, keepdims=True))
            cross.append(jnp.sum(sx * kx, axis=0, keepdims=True))
    sums = jnp.sum(jnp.concatenate(power + cross, axis=0), axis=1, keepdims=True)
    ratio = sums[states:] / (sums[:states] + EPS)
    for s in range(states):
        resid = kx_ref[:, s] - ratio[s : s + 1][None] * sx_ref[:, s]
        resid = resid.reshape(half, width)
        norm.append(jnp.sum(resid * resid, axis=0, keepdims=True))
    norm = jnp.sum(jnp.concatenate(norm, axis=0), axis=1, keepdims=True)
    column = jnp.concatenate([sums, norm], axis=0)
    shape = (3 * states, width)
    mine = lax.broadcasted_iota(jnp.int32, shape, 0) == lax.broadcasted_iota(jnp.int32, shape, 1)
    row = jnp.sum(jnp.where(mine, jnp.broadcast_to(column, shape), 0.0), axis=0, keepdims=True)
    stat_ref[...] = jnp.broadcast_to(row[None], stat_ref.shape)


def merge_kernel(states, parts_ref, stat_ref):
    power, cross, norm, _ = merged_rows(parts_ref[...].reshape(parts_ref.shape[0], -1), states)
    stat_ref[...] = jnp.broadcast_to(packed(power, cross, norm, states)[None], stat_ref.shape)


def final_kernel(states, cells, parts_ref, kx_ref, sx_ref, out_ref, ritz_ref):
    _, _, norm, ritz = merged_rows(parts_ref[...].reshape(parts_ref.shape[0], -1), states)
    scale = lax.rsqrt(norm / cells + EPS)
    for s in range(states):
        out_ref[:, s] = (kx_ref[:, s] - pick(ritz, s)[None] * sx_ref[:, s]) * pick(scale, s)[None]
        ritz_ref[s] = ritz[0, s]


def led(group, lead):
    return [lead] + [m for m in group if m != lead]


def sum_phases(rows, cols, layers):
    lines = [
        led([row * cols + c for row in (x, x + 1) for c in range(cols)], (x + 1) * cols + cols // 2 + 1)
        for x in range(0, rows, 2)
    ]
    planes = [
        led(
            [row * layers + m for row in range(core, rows, 2) for m in range(layers)],
            (rows - 2 + core) * layers + layers // 2,
        )
        for core in range(2)
    ]
    return [(("row", "col"), lines), (("row", "state"), planes)]


def per_device(vectors, onsite, k_tiles, s_tiles, columns, counts):
    rows_blk, states, width, _ = vectors.shape
    layers = lax.axis_size("state")
    layer = lax.axis_index("state")
    own = width // layers
    slot_dev = k_tiles.shape[1]
    device = lax.axis_index(("row", "col"))
    window = rows_blk + 2 * REACH

    count = lax.axis_size(("row", "col"))
    forward = [(i, i + 1) for i in range(count - 1)]
    backward = [(b, a) for a, b in forward]
    low = lax.ppermute(vectors[rows_blk - REACH :], ("row", "col"), forward)
    high = lax.ppermute(vectors[:REACH], ("row", "col"), backward)

    half = layers // 2
    order = [k // 2 + (half if k % 2 == 0 else 0) for k in range(layers)]
    send = pl.pallas_call(
        functools.partial(send_kernel, order),
        out_shape=jax.ShapeDtypeStruct((layers, 2, rows_blk, slot_dev, own, width), k_tiles.dtype),
        in_specs=[ANY, ANY],
        out_specs=ANY,
        scratch_shapes=[
            pltpu.VMEM((layers, 2, rows_blk, slot_dev, own, width), k_tiles.dtype),
            pltpu.SemaphoreType.DMA((layers, 2)),
            pltpu.SemaphoreType.DMA((layers, 2)),
        ],
        compiler_params=limit(8),
    )(*(pltpu.with_memory_space_constraint(t, pltpu.HBM) for t in (k_tiles, s_tiles)))
    tiles = lax.all_to_all(
        send, "state", 0, 0, axis_index_groups=[order], tiled=True
    )

    spot = jnp.stack([device * rows_blk - REACH, layer])
    tall = 2 * rows_blk * own
    total, oper = pl.pallas_call(
        functools.partial(early_kernel, states, order),
        out_shape=(
            jax.ShapeDtypeStruct((tall, states * width), jnp.float32),
            jax.ShapeDtypeStruct((tall, (window + 1) * width), vectors.dtype),
        ),
        in_specs=[SMEM] * 3 + [VMEM] * 4,
        out_specs=(VMEM, VMEM),
        compiler_params=limit(12),
    )(spot, columns, counts, tiles, low, vectors, onsite)

    phases = sum_phases(lax.axis_size("row"), lax.axis_size("col"), layers)
    inner, outer = (len(groups[0]) for _, groups in phases)
    outs = jax.ShapeDtypeStruct((rows_blk, states, own, width), jnp.float32)
    kx, sx, stat = pl.pallas_call(
        functools.partial(late_kernel, states),
        out_shape=(outs, outs, jax.ShapeDtypeStruct((inner, 1, width), jnp.float32)),
        in_specs=[VMEM] * 3,
        out_specs=(VMEM, VMEM, VMEM),
        compiler_params=limit(12),
    )(total, oper, high)

    axes, groups = phases[0]
    stat = lax.all_to_all(stat, axes, 0, 0, axis_index_groups=groups, tiled=True)
    stat = pl.pallas_call(
        functools.partial(merge_kernel, states),
        out_shape=jax.ShapeDtypeStruct((outer, 1, width), jnp.float32),
        in_specs=[VMEM],
        out_specs=VMEM,
        compiler_params=limit(2),
    )(stat)
    axes, groups = phases[1]
    stat = lax.all_to_all(stat, axes, 0, 0, axis_index_groups=groups, tiled=True)
    correction, ritz = pl.pallas_call(
        functools.partial(final_kernel, states, count * rows_blk * width * width),
        out_shape=(outs, jax.ShapeDtypeStruct((states,), jnp.float32)),
        in_specs=[VMEM] * 3,
        out_specs=(VMEM, SMEM),
        compiler_params=limit(4),
    )(stat, kx, sx)
    return correction, ritz


def solution(mesh):
    placed = (
        P(("row", "col"), None, None, None),
        P(("row", "col"), "state"),
        P(("row", "col"), "state", None, None),
        P(("row", "col"), "state", None, None),
        P(("row", "col"), None),
        P(("row", "col")),
    )
    return jax.shard_map(
        per_device,
        mesh=mesh,
        in_specs=placed,
        out_specs=(P(("row", "col"), None, "state", None), P()),
        check_vma=False,
    )
```
